1024 devices in a mesh: band: 16 (over z_hi, x), tr: 8 (over z_lo, core), tc: 8 (over y).
Axes of the slice: x: 4, y: 8, z: 16 (z_hi: 4, z_lo: 4; z = z_hi * 4 + z_lo), core: 2. Of those that a mesh axis runs over, the one named last changes fastest.
Arguments:
- voltages: bfloat16 [131072, 2, 1024], P(('band', 'tr', 'tc')), parts along dimension 0, may hold values from -4 to 4
Outputs:
- visibilities: bfloat16 [512, 2, 1024, 1024], P(('band', 'tc'), None, 'tr'), parts along dimension 0
The draws below stay inside these ranges and needn't reach their ends.
There are 16 independent parts, one for each index of `band`. The reference program is written for one: setup_inputs(seed, part) draws one part's arguments, and reference() takes and returns one part's arrays. A program takes and returns all parts, laid end to end along the dimension named above; each array names one. Nothing has to cross between parts.
All inputs are finite; a program needn't handle non-finite values.
Results may differ from the reference program's by a relative error of at most 0.0054.
Values may be sent and summed in bfloat16 or wider, within the bound.
A program may use at most 32 MiB of HBM per device.

```python
import math
import jax
import jax.numpy as jnp
from jax import lax

INPUTS = 1024
FINE = 32
TAPS = 16
SPECTRA = 256
SAMPLES = 8192


def level_of(rng, dims, shards, smallest, largest):
    def one(dim, shards_of):
        draws = jax.random.uniform(jax.random.fold_in(jax.random.fold_in(rng, 6), dim), (shards_of,), jnp.float32, smallest / len(shards), largest / len(shards))
        return jnp.repeat(jnp.exp(draws), dims[dim] // shards_of).reshape((-1,) + (1,) * (len(dims) - dim - 1))

    level = one(*shards[0])
    for cut in shards[1:]:
        level = level * one(*cut)
    return level


def noise(rng, extent, spread, bound, pieces=(), kind=jnp.bfloat16):
    gain = level_of(rng, extent, pieces, -0.22, 0.18) if pieces else 1.0
    array = jax.random.normal(rng, extent, jnp.float32) * spread * gain
    return jnp.minimum(jnp.maximum(array, -bound), bound).astype(kind)


def setup_inputs(seed: int = 0, part: int = 0) -> dict:
    splits = jax.random.split(jax.random.key(seed), 2)
    part_splits = jax.random.split(jax.random.fold_in(splits[1], part), 2)
    return {
        "voltages": noise(part_splits[0], (SAMPLES, 2, INPUTS), 1.0, 4.0, ((0, 64),)),
    }


def filter_taps(tap_total, fine_total):
    length = tap_total * fine_total
    position = jnp.arange(length).astype(jnp.float32)
    offset = (position - (length - 1) / 2.0) / fine_total
    prototype = jnp.sin(math.pi * offset) / (math.pi * offset)
    prototype = prototype / jnp.sqrt(jnp.sum(prototype * prototype))
    return prototype.reshape(tap_total, fine_total)

def fourier_table(fine_total):
    indices = jnp.arange(fine_total).astype(jnp.float32)
    angles = 2.0 * math.pi * jnp.mod(indices[:, None] * indices[None, :], fine_total) / fine_total
    cosine = jnp.cos(angles)
    sine_part = jnp.sin(angles)
    stacked = jnp.stack([jnp.stack([cosine, -sine_part], axis=-1), jnp.stack([sine_part, cosine], axis=-1)], axis=1)
    return stacked.reshape(2 * fine_total, 2 * fine_total)

def reference(voltages):
    tap_table = filter_taps(TAPS, FINE)
    fourier = fourier_table(FINE)
    leading = jnp.zeros(((TAPS - 1) * FINE, 2, INPUTS), voltages.dtype)
    padded = jnp.concatenate([leading, voltages], axis=0).reshape(SPECTRA + TAPS - 1, FINE, 2, INPUTS)
    weighted = jnp.zeros((SPECTRA, FINE, 2, INPUTS), jnp.float32)
    for tap_index in range(TAPS):
        weighted = weighted + tap_table[tap_index][None, :, None, None] * padded[tap_index:tap_index + SPECTRA].astype(jnp.float32)
    spectra = jnp.einsum('sjm,jo->som', weighted.reshape(SPECTRA, 2 * FINE, INPUTS), fourier, precision=lax.Precision.HIGHEST)
    spectra = spectra.reshape(SPECTRA, FINE, 2, INPUTS).astype(jnp.bfloat16)
    channel_major = jnp.transpose(spectra, (1, 0, 2, 3)).astype(jnp.float32)

    def one_channel(channel_block):
        swapped = jnp.stack([channel_block[:, 1], -channel_block[:, 0]], axis=1)
        stacked = jnp.stack([channel_block, swapped], axis=0)
        return jnp.einsum('rsci,scj->rij', stacked, channel_block, precision=lax.Precision.HIGHEST)
    summed = lax.map(one_channel, channel_major)
    return (summed / float(SPECTRA)).astype(jnp.bfloat16)
```

```python
import math

import jax
import jax.numpy as jnp
import ml_dtypes
import numpy as np
from jax import lax
from jax.experimental import pallas as pl
from jax.experimental.pallas import tpu as pltpu
from jax.sharding import PartitionSpec as P

MESH = pl.DeviceIdType.MESH
BF16 = jnp.bfloat16
F32 = jnp.float32

FINE = 32
TAPS = 16
LANES = 128
TC = 8
LINE = 4
CORES = 2
KK = FINE // TC
HOPS = 4
ROWS = HOPS * FINE * 2
OLD = 4
WINDOW = 6
HALF = 16
OFF = (0, 1, 7, 2, 6, 3, 5, 4)


def filter_constant():
    length = TAPS * FINE
    offset = (np.arange(length) - (length - 1) / 2.0) / FINE
    prototype = np.sin(math.pi * offset) / (math.pi * offset)
    taps = (prototype / np.sqrt(np.sum(prototype * prototype))).reshape(TAPS, FINE)
    index = np.arange(FINE)
    angle = 2.0 * math.pi * np.mod(index[:, None] * index[None, :], FINE) / FINE
    cosine, sine = np.cos(angle), np.sin(angle)
    fourier = np.zeros((FINE, 2, FINE, 2))
    fourier[:, 0, :, 0] = cosine
    fourier[:, 1, :, 0] = sine
    fourier[:, 0, :, 1] = -sine
    fourier[:, 1, :, 1] = cosine
    table = np.zeros((FINE, 2, 8, WINDOW * HOPS, FINE, 2))
    for s in range(8):
        for t in range(TAPS):
            table[:, :, s, s + 1 + t] = np.transpose(taps[t][:, None, None, None] * fourier, (2, 3, 0, 1))
    table = table.reshape(FINE * 2 * 8, WINDOW * ROWS).astype(np.float32)
    high = table.astype(ml_dtypes.bfloat16)
    low = (table - high.astype(np.float32)).astype(ml_dtypes.bfloat16)
    cut = FINE * 2 * 8 // 2
    return np.stack([np.concatenate([high[i * cut:(i + 1) * cut], low[i * cut:(i + 1) * cut]]) for i in range(2)])


def kernel(x_ref, g_hbm, out_ref, g_ref, raw, s_ref, r1, r0,
           g_sem, own_sem, ring_send, ring_recv, halo_send, halo_recv,
           turn1_send, turn1_recv, turn0_send, turn0_recv, own1_sem, own0_sem,
           line1_send, line1_recv, line0_send, line0_recv,
           pair1_send, pair1_recv, pair0_send, pair0_recv):
    tr = lax.axis_index("tr")
    y = lax.axis_index("tc")
    core = lax.rem(tr, 2)
    zl = tr // 2
    other = 1 - core
    sibling = zl * 2 + other

    table = pltpu.make_async_copy(g_hbm, g_ref, g_sem)
    table.start()

    def at(q, sign):
        return lax.rem(y + sign * OFF[q] + TC, TC)

    barrier = pltpu.get_barrier_semaphore()

    def greet(t, c):
        pl.semaphore_signal(barrier, inc=1, device_id={"tr": t, "tc": c}, device_id_type=MESH)

    for q in range(1, TC):
        greet(tr, at(q, -1))
    greet(sibling, y)

    @pl.when(zl > 0)
    def _():
        greet(tr - 2, y)

    @pl.when(zl < LINE - 1)
    def _():
        greet(tr + 2, y)

    @pl.when((core == 1) & (zl < LINE - 1))
    def _():
        greet(tr + 1, y)

    @pl.when((core == 0) & (zl > 0))
    def _():
        greet(tr - 1, y)

    inner = (zl > 0).astype(jnp.int32) + (zl < LINE - 1).astype(jnp.int32)
    halo_peer = jnp.where(core == 1, (zl < LINE - 1).astype(jnp.int32), (zl > 0).astype(jnp.int32))
    pl.semaphore_wait(barrier, TC + inner + halo_peer)

    def remote(src, dst, send, recv, t, c):
        return pltpu.make_async_remote_copy(
            src_ref=src, dst_ref=dst, send_sem=send, recv_sem=recv,
            device_id={"tr": t, "tc": c}, device_id_type=MESH)

    for q in range(TC - 1, 0, -1):
        c = at(q, -1)
        remote(x_ref.at[c], raw.at[OLD + y], ring_send, ring_recv, tr, c).start()
    own = pltpu.make_async_copy(x_ref.at[y], raw.at[OLD + y], own_sem)
    own.start()

    @pl.when(tr == 0)
    def _():
        raw[0:OLD] = jnp.zeros((OLD, ROWS, LANES), BF16)

    own.wait()
    arrivals = remote(x_ref.at[pl.ds(0, TC - 1)], raw.at[pl.ds(OLD, TC - 1)], ring_send, ring_recv, tr, y)
    arrivals.wait_recv()

    last = 2 * LINE - 1
    halo = remote(raw.at[pl.ds(TC, OLD)], raw.at[pl.ds(0, OLD)], halo_send, halo_recv, jnp.minimum(tr + 1, last), y)

    @pl.when(tr < last)
    def _():
        halo.start()

    table.wait()

    def filterbank(half):
        first = HOPS * half
        window = jnp.concatenate(
            [raw[first:first + WINDOW].reshape(WINDOW * ROWS, LANES),
             raw[first + 2:first + 2 + WINDOW].reshape(WINDOW * ROWS, LANES)], axis=1)
        for part in range(2):
            both = jnp.dot(g_ref[part], window, preferred_element_type=F32)
            count = both.shape[0] // 2
            total = both[:count] + both[count:]
            pair = jnp.concatenate(
                [total[:, :LANES].reshape(count // 8, 8, LANES), total[:, LANES:].reshape(count // 8, 8, LANES)],
                axis=1)
            s_ref[half, part * (TC // 2):(part + 1) * (TC // 2)] = pair.astype(BF16).reshape(
                TC // 2, KK, 2, HALF, LANES)

    filterbank(1)
    own1 = pltpu.make_async_copy(s_ref.at[1, y], r1.at[core, zl, y], own1_sem)
    own1.start()
    for q in range(1, TC):
        c = at(q, -1)
        remote(s_ref.at[1, c], r1.at[core, zl, y], turn1_send, turn1_recv.at[q], tr, c).start()

    def spread(r, s, piece, line_send, line_recv, pair_send, pair_recv, rightward, leftward):
        src = piece(r, s)
        if rightward:
            @pl.when(zl < LINE - 1)
            def _():
                remote(src, src, line_send.at[0, s], line_recv, jnp.minimum(tr + 2, last), y).start()
        if leftward:
            @pl.when(zl > 0)
            def _():
                remote(src, src, line_send.at[1, s], line_recv, jnp.maximum(tr - 2, 0), y).start()
        remote(src, src, pair_send.at[s], pair_recv, sibling, y).start()

    def piece1(q):
        return lambda r, s: r.at[core, s, at(q, 1)]

    def piece0(k):
        return lambda r, s: r.at[core, s, k]

    def from_line(i, dist, pieces, r, piece_of, line_send, line_recv, pair_send, pair_recv_of):
        p = i - dist
        if p < 0 or p >= pieces:
            return

        @pl.when(zl >= dist)
        def _():
            s = jnp.maximum(zl - dist, 0)
            piece = piece_of(p)
            remote(piece(r, s), piece(r, s), line_send.at[0, s], line_recv.at[s, p], sibling, y).wait_recv()
            spread(r, s, piece, line_send, line_recv.at[s, p], pair_send, pair_recv_of(s, p), True, False)

        @pl.when(zl < LINE - dist)
        def _():
            s = jnp.minimum(zl + dist, LINE - 1)
            piece = piece_of(p)
            remote(piece(r, s), piece(r, s), line_send.at[1, s], line_recv.at[s, p], sibling, y).wait_recv()
            spread(r, s, piece, line_send, line_recv.at[s, p], pair_send, pair_recv_of(s, p), False, True)

    def pair1_of(s, p):
        return pair1_recv

    def pair0_of(s, p):
        return pair0_recv.at[p]

    for i in range(TC + LINE - 1):
        if i < TC:
            piece = piece1(i)
            if i == 0:
                own1.wait()
            else:
                c = at(i, 1)
                remote(s_ref.at[1, 0], r1.at[core, zl, c], turn1_send, turn1_recv.at[i], sibling, y).wait_recv()
            spread(r1, zl, piece, line1_send, line1_recv.at[zl, i], pair1_send, pair1_recv, True, True)
        for dist in range(1, LINE):
            from_line(i, dist, TC, r1, piece1, line1_send, line1_recv, pair1_send, pair1_of)
        if i == 0:
            @pl.when(tr > 0)
            def _():
                halo.wait_recv()

            filterbank(0)
            own0 = pltpu.make_async_copy(s_ref.at[0, y], r0.at[core, zl, :, y], own0_sem)
            own0.start()
            for q in range(1, TC):
                c = at(q, -1)
                remote(s_ref.at[0, c], r0.at[core, zl, :, y], turn0_send, turn0_recv, tr, c).start()

    own0.wait()
    remote(r0.at[core, zl, :, pl.ds(0, TC - 1)], r0.at[core, zl, :, pl.ds(0, TC - 1)],
           turn0_send, turn0_recv, sibling, y).wait_recv()

    def correlate(k):
        def block(b):
            return jnp.concatenate(
                [r1[:, :, b, k].reshape(TC * 2 * HALF, LANES), r0[:, :, k, b].reshape(TC * 2 * HALF, LANES)], axis=0)

        mine = jnp.concatenate([r1[:, :, tr, k], r0[:, :, k, tr]], axis=0)
        swapped = jnp.concatenate([mine[:, :, 1:2], -mine[:, :, 0:1]], axis=2)
        depth = 2 * TC * 2 * HALF
        left = jnp.concatenate([mine.reshape(depth, LANES), swapped.reshape(depth, LANES)], axis=1)
        right = jnp.concatenate([block(b) for b in range(TC)], axis=1)
        product = lax.dot_general(left, right, (((0,), (0,)), ((), ())), preferred_element_type=F32)
        product = product * (1.0 / (LINE * CORES * 2 * HALF))
        out_ref[k] = product.astype(BF16).reshape(2, LANES, TC * LANES)

    def tail_waits():
        table_half = s_ref.at[1, pl.ds(0, TC - 1)]
        arrivals.wait_send()

        @pl.when(tr < last)
        def _():
            halo.wait_send()

        remote(table_half, table_half, turn1_send, turn1_recv.at[0], sibling, y).wait_send()
        remote(table_half, table_half, turn0_send, turn0_recv, sibling, y).wait_send()
        sent_waits(r1, line1_send, pair1_send)
        remote(r1.at[other], r1.at[other], pair1_send.at[0], pair1_recv, sibling, y).wait_recv()

    def sent_waits(r, line_send, pair_send):
        for s in range(LINE):
            whole = r.at[core, s]

            @pl.when((zl < LINE - 1) & (s <= zl))
            def _():
                remote(whole, whole, line_send.at[0, s], pair0_recv.at[0], sibling, y).wait_send()

            @pl.when((zl > 0) & (s >= zl))
            def _():
                remote(whole, whole, line_send.at[1, s], pair0_recv.at[0], sibling, y).wait_send()

            remote(whole, whole, pair_send.at[s], pair0_recv.at[0], sibling, y).wait_send()

    for i in range(KK + LINE - 1):
        if i < KK:
            spread(r0, zl, piece0(i), line0_send, line0_recv.at[zl, i], pair0_send, pair0_recv.at[i], True, True)
        if i == KK - 1:
            tail_waits()
        for dist in range(1, LINE):
            from_line(i, dist, KK, r0, piece0, line0_send, line0_recv, pair0_send, pair0_of)
        k = i - (LINE - 1)
        if k >= 0:
            theirs = r0.at[other, :, k]
            remote(theirs, theirs, pair0_send.at[0], pair0_recv.at[k], sibling, y).wait_recv()
            correlate(k)
    sent_waits(r0, line0_send, pair0_send)


def per_device(voltages):
    samples, _, inputs = voltages.shape
    blocks = inputs // LANES
    x = voltages.reshape(samples, 2, blocks, LANES).transpose(2, 0, 1, 3).reshape(blocks, samples * 2, LANES)
    table = jnp.asarray(filter_constant())
    any_spec = pl.BlockSpec(memory_space=pl.ANY)
    dma = pltpu.SemaphoreType.DMA
    return pl.pallas_call(
        kernel,
        out_shape=jax.ShapeDtypeStruct((KK, 2, LANES, inputs), BF16),
        in_specs=[any_spec, pl.BlockSpec(memory_space=pltpu.HBM)],
        out_specs=pl.BlockSpec(memory_space=pltpu.VMEM),
        scratch_shapes=[
            pltpu.VMEM(table.shape, BF16),
            pltpu.VMEM((OLD + TC, ROWS, LANES), BF16),
            pltpu.VMEM((2, TC, KK, 2, HALF, LANES), BF16),
            pltpu.VMEM((CORES, LINE, TC, KK, 2, HALF, LANES), BF16),
            pltpu.VMEM((CORES, LINE, KK, TC, 2, HALF, LANES), BF16),
            dma, dma, dma, dma, dma, dma,
            dma, dma((TC,)), dma, dma, dma, dma,
            dma((2, LINE)), dma((LINE, TC)), dma((2, LINE)), dma((LINE, KK)),
            dma((LINE,)), dma, dma((LINE,)), dma((KK,)),
        ],
        compiler_params=pltpu.CompilerParams(
            collective_id=0, has_side_effects=True, vmem_limit_bytes=51 * 1024 * 1024),
    )(x, table)


def solution(mesh):
    return jax.shard_map(
        per_device,
        mesh=mesh,
        in_specs=(P(("band", "tr", "tc"), None, None),),
        out_specs=P(("band", "tc"), None, "tr", None),
        check_vma=False,
    )
```

```python
import math

import jax
import jax.numpy as jnp
import ml_dtypes
import numpy as np
from jax import lax
from jax.experimental import pallas as pl
from jax.experimental.pallas import tpu as pltpu
from jax.sharding import PartitionSpec as P

MESH = pl.DeviceIdType.MESH
BF16 = jnp.bfloat16
F32 = jnp.float32

FINE = 32
TAPS = 16
LANES = 128
TC = 8
LINE = 4
CORES = 2
KK = FINE // TC
HOPS = 4
ROWS = HOPS * FINE * 2
OLD = 4
WINDOW = 6
HALF = 16
PART = 4
OFF = (0, 1, 7, 2, 6, 3, 5, 4)
UNITS = TC + KK
LAG = (2, 4, 6)
ORDER = ((0, 0), (TC - 1, 2))


def filter_constant():
    length = TAPS * FINE
    offset = (np.arange(length) - (length - 1) / 2.0) / FINE
    prototype = np.sin(math.pi * offset) / (math.pi * offset)
    taps = (prototype / np.sqrt(np.sum(prototype * prototype))).reshape(TAPS, FINE)
    index = np.arange(FINE)
    angle = 2.0 * math.pi * np.mod(index[:, None] * index[None, :], FINE) / FINE
    cosine, sine = np.cos(angle), np.sin(angle)
    fourier = np.zeros((FINE, 2, FINE, 2))
    fourier[:, 0, :, 0] = cosine
    fourier[:, 1, :, 0] = sine
    fourier[:, 0, :, 1] = -sine
    fourier[:, 1, :, 1] = cosine
    table = np.zeros((FINE, 2, 8, WINDOW * HOPS, FINE, 2))
    for s in range(8):
        for t in range(TAPS):
            table[:, :, s, s + 1 + t] = np.transpose(taps[t][:, None, None, None] * fourier, (2, 3, 0, 1))
    table = table.reshape(FINE * 2 * 8, WINDOW * ROWS).astype(np.float32)
    high = table.astype(ml_dtypes.bfloat16)
    low = (table - high.astype(np.float32)).astype(ml_dtypes.bfloat16)
    return np.concatenate([high.reshape(TC, -1, WINDOW * ROWS), low.reshape(TC, -1, WINDOW * ROWS)], axis=1)


def kernel(x_ref, g_hbm, out_ref, g_ref, raw, s_ref, r1, r0,
           g_sem, own_sem, ring_send, ring_recv, halo_send, halo_recv,
           turn1_send, turn1_recv, turn0_send, turn0_recv, own1_sem, own0_sem,
           line1_send, line1_recv, line0_send, line0_recv,
           pair1_send, pair1_recv, pair0_send, pair0_recv,
           line_ok, pair_ok, halo_ok):
    tr = lax.axis_index("tr")
    y = lax.axis_index("tc")
    core = lax.rem(tr, 2)
    zl = tr // 2
    other = 1 - core
    sibling = zl * 2 + other

    table = pltpu.make_async_copy(g_hbm, g_ref, g_sem)
    table.start()

    def at(q, sign):
        return lax.rem(y + sign * OFF[q] + TC, TC)

    barrier = pltpu.get_barrier_semaphore()

    def greet(t, c):
        pl.semaphore_signal(barrier, inc=1, device_id={"tr": t, "tc": c}, device_id_type=MESH)

    for q in range(1, TC):
        greet(tr, at(q, -1))
    last = 2 * LINE - 1
    below = (zl > 0).astype(jnp.int32)
    above = (zl < LINE - 1).astype(jnp.int32)

    @pl.when(core == 1)
    def _():
        @pl.when(zl < LINE - 1)
        def _():
            greet(jnp.minimum(tr + 2, last), y)
            greet(jnp.minimum(tr + 1, last), y)

    @pl.when(core == 0)
    def _():
        @pl.when(zl > 0)
        def _():
            greet(jnp.maximum(tr - 2, 0), y)

    pl.semaphore_wait(barrier, TC - 1 + jnp.where(core == 1, below, 1 + above + below))

    def tell(sem, t):
        pl.semaphore_signal(sem, inc=1, device_id={"tr": t, "tc": y}, device_id_type=MESH)

    @pl.when(core == 1)
    def _():
        @pl.when(zl > 0)
        def _():
            tell(line_ok, jnp.maximum(tr - 2, 0))

    @pl.when(core == 0)
    def _():
        tell(pair_ok, sibling)

        @pl.when(zl > 0)
        def _():
            tell(halo_ok, jnp.maximum(tr - 1, 0))

        @pl.when(zl < LINE - 1)
        def _():
            tell(line_ok, jnp.minimum(tr + 2, last))

    def remote(src, dst, send, recv, t, c):
        return pltpu.make_async_remote_copy(
            src_ref=src, dst_ref=dst, send_sem=send, recv_sem=recv,
            device_id={"tr": t, "tc": c}, device_id_type=MESH)

    for q in range(TC - 1, 0, -1):
        c = at(q, -1)
        remote(x_ref.at[c], raw.at[OLD + y], ring_send, ring_recv, tr, c).start()
    own = pltpu.make_async_copy(x_ref.at[y], raw.at[OLD + y], own_sem)
    own.start()

    @pl.when(tr == 0)
    def _():
        raw[0:OLD] = jnp.zeros((OLD, ROWS, LANES), BF16)

    own.wait()
    arrivals = remote(x_ref.at[pl.ds(0, TC - 1)], raw.at[pl.ds(OLD, TC - 1)], ring_send, ring_recv, tr, y)
    arrivals.wait_send()

    @pl.when(core == 1)
    def _():
        greet(sibling, y)

    arrivals.wait_recv()

    halo = remote(raw.at[pl.ds(TC, OLD)], raw.at[pl.ds(0, OLD)], halo_send, halo_recv, jnp.minimum(tr + 1, last), y)

    @pl.when((core == 1) & (tr < last))
    def _():
        pl.semaphore_wait(halo_ok, 1)

    @pl.when(tr < last)
    def _():
        halo.start()

    table.wait()

    def filterbank(half, after):
        first = HOPS * half
        window = jnp.concatenate(
            [raw[first:first + WINDOW].reshape(WINDOW * ROWS, LANES),
             raw[first + 2:first + 2 + WINDOW].reshape(WINDOW * ROWS, LANES)], axis=1)
        for part in range(2):
            groups = [at(q, -1) for q in range(part * PART, (part + 1) * PART)]
            both = jnp.dot(jnp.concatenate([g_ref[c] for c in groups], axis=0), window, preferred_element_type=F32)
            both = both.reshape(PART, 2, KK * 2, 8, 2 * LANES)
            total = both[:, 0] + both[:, 1]
            pair = jnp.concatenate([total[..., :LANES], total[..., LANES:]], axis=2).astype(BF16)
            for j, c in enumerate(groups):
                s_ref[half, c] = pair[j].reshape(KK, 2, HALF, LANES)
            after(part)

    own1 = pltpu.make_async_copy(s_ref.at[1, y], r1.at[core, zl, y], own1_sem)

    def turn_second(part):
        for q in range(part * PART, (part + 1) * PART):
            if q == 0:
                own1.start()
            else:
                c = at(q, -1)
                remote(s_ref.at[1, c], r1.at[core, zl, y], turn1_send, turn1_recv.at[q], tr, c).start()

    filterbank(1, turn_second)

    def spread(r, s, piece, line_send, line_recv, pair_send, pair_recv, rightward, leftward):
        src = piece(r, s)
        if rightward:
            @pl.when(zl < LINE - 1)
            def _():
                remote(src, src, line_send.at[0, s], line_recv, jnp.minimum(tr + 2, last), y).start()
        if leftward:
            @pl.when(zl > 0)
            def _():
                remote(src, src, line_send.at[1, s], line_recv, jnp.maximum(tr - 2, 0), y).start()
        remote(src, src, pair_send.at[s], pair_recv, sibling, y).start()

    def piece1(q):
        return lambda r, s: r.at[core, s, at(q, 1)]

    def piece0(k):
        return lambda r, s: r.at[core, s, k]

    def from_line(dist, p, r, piece_of, line_send, line_recv, pair_send, pair_recv_of):
        @pl.when(zl >= dist)
        def _():
            s = jnp.maximum(zl - dist, 0)
            piece = piece_of(p)
            remote(piece(r, s), piece(r, s), line_send.at[0, s], line_recv.at[s, p], sibling, y).wait_recv()
            spread(r, s, piece, line_send, line_recv.at[s, p], pair_send, pair_recv_of(s, p), True, False)

        @pl.when(zl < LINE - dist)
        def _():
            s = jnp.minimum(zl + dist, LINE - 1)
            piece = piece_of(p)
            remote(piece(r, s), piece(r, s), line_send.at[1, s], line_recv.at[s, p], sibling, y).wait_recv()
            spread(r, s, piece, line_send, line_recv.at[s, p], pair_send, pair_recv_of(s, p), False, True)

    def pair1_of(s, p):
        return pair1_recv

    def pair0_of(s, p):
        return pair0_recv.at[p]

    def first_half():
        @pl.when(tr > 0)
        def _():
            halo.wait_recv()

        filterbank(0, lambda part: None)
        own0.start()
        for k in range(KK):
            for q in range(1, TC):
                c = at(q, -1)
                remote(s_ref.at[0, c, k], r0.at[core, zl, k, y], turn0_send, turn0_recv.at[k], tr, c).start()

    own0 = pltpu.make_async_copy(s_ref.at[0, y], r0.at[core, zl, :, y], own0_sem)

    def correlate(k):
        def block(b):
            return jnp.concatenate(
                [r1[:, :, b, k].reshape(TC * 2 * HALF, LANES), r0[:, :, k, b].reshape(TC * 2 * HALF, LANES)], axis=0)

        mine = jnp.concatenate([r1[:, :, tr, k], r0[:, :, k, tr]], axis=0)
        swapped = jnp.concatenate([mine[:, :, 1:2], -mine[:, :, 0:1]], axis=2)
        depth = 2 * TC * 2 * HALF
        left = jnp.concatenate([mine.reshape(depth, LANES), swapped.reshape(depth, LANES)], axis=1)
        right = jnp.concatenate([block(b) for b in range(TC)], axis=1)
        product = lax.dot_general(left, right, (((0,), (0,)), ((), ())), preferred_element_type=F32)
        product = product * (1.0 / (LINE * CORES * 2 * HALF))
        out_ref[k] = product.astype(BF16).reshape(2, LANES, TC * LANES)

    def tail_waits():
        table_half = s_ref.at[1, pl.ds(0, TC - 1)]
        @pl.when(tr < last)
        def _():
            halo.wait_send()

        remote(table_half, table_half, turn1_send, turn1_recv.at[0], sibling, y).wait_send()
        remote(table_half, table_half, turn0_send, turn0_recv.at[0], sibling, y).wait_send()
        sent_waits(r1, line1_send, pair1_send)
        remote(r1.at[other], r1.at[other], pair1_send.at[0], pair1_recv, sibling, y).wait_recv()

    def sent_waits(r, line_send, pair_send):
        for s in range(LINE):
            whole = r.at[core, s]

            @pl.when((zl < LINE - 1) & (s <= zl))
            def _():
                remote(whole, whole, line_send.at[0, s], pair0_recv.at[0], sibling, y).wait_send()

            @pl.when((zl > 0) & (s >= zl))
            def _():
                remote(whole, whole, line_send.at[1, s], pair0_recv.at[0], sibling, y).wait_send()

            remote(whole, whole, pair_send.at[s], pair0_recv.at[0], sibling, y).wait_send()

    def take_own(u):
        if u < TC:
            if u == 0:
                own1.wait()
            else:
                c = at(u, 1)
                remote(s_ref.at[1, 0], r1.at[core, zl, c], turn1_send, turn1_recv.at[u], sibling, y).wait_recv()
            spread(r1, zl, piece1(u), line1_send, line1_recv.at[zl, u], pair1_send, pair1_recv, True, True)
            return
        k = u - TC
        if k == 0:
            own0.wait()
        seven = r0.at[core, zl, k, pl.ds(0, TC - 1)]
        remote(seven, seven, turn0_send, turn0_recv.at[k], sibling, y).wait_recv()
        spread(r0, zl, piece0(k), line0_send, line0_recv.at[zl, k], pair0_send, pair0_recv.at[k], True, True)

    def take_line(dist, u):
        if u < TC:
            from_line(dist, u, r1, piece1, line1_send, line1_recv, pair1_send, pair1_of)
        else:
            from_line(dist, u - TC, r0, piece0, line0_send, line0_recv, pair0_send, pair0_of)

    @pl.when(((core == 1) & (zl < LINE - 1)) | ((core == 0) & (zl > 0)))
    def _():
        pl.semaphore_wait(line_ok, 1)

    @pl.when(core == 1)
    def _():
        pl.semaphore_wait(pair_ok, 1)

    def run(first_at, gap):
        place = [u if u < TC else u + gap for u in range(UNITS)]
        for i in range(place[-1] + LAG[2] + 1):
            for u in range(UNITS):
                if place[u] == i:
                    take_own(u)
            if i == first_at:
                first_half()
            for dist in range(1, LINE):
                for u in range(UNITS):
                    if place[u] + LAG[dist - 1] == i:
                        take_line(dist, u)
            for k in range(KK):
                if place[TC + k] + LAG[2] == i:
                    if k == 0:
                        tail_waits()
                    theirs = r0.at[other, :, k]
                    remote(theirs, theirs, pair0_send.at[0], pair0_recv.at[k], sibling, y).wait_recv()
                    correlate(k)

    @pl.when(core == 1)
    def _():
        run(*ORDER[1])

    @pl.when(core == 0)
    def _():
        run(*ORDER[0])

    sent_waits(r0, line0_send, pair0_send)


def per_device(voltages):
    samples, _, inputs = voltages.shape
    blocks = inputs // LANES
    x = voltages.reshape(samples, 2, blocks, LANES).transpose(2, 0, 1, 3).reshape(blocks, samples * 2, LANES)
    table = jnp.asarray(filter_constant())
    any_spec = pl.BlockSpec(memory_space=pl.ANY)
    dma = pltpu.SemaphoreType.DMA
    return pl.pallas_call(
        kernel,
        out_shape=jax.ShapeDtypeStruct((KK, 2, LANES, inputs), BF16),
        in_specs=[any_spec, pl.BlockSpec(memory_space=pltpu.HBM)],
        out_specs=pl.BlockSpec(memory_space=pltpu.VMEM),
        scratch_shapes=[
            pltpu.VMEM(table.shape, BF16),
            pltpu.VMEM((OLD + TC, ROWS, LANES), BF16),
            pltpu.VMEM((2, TC, KK, 2, HALF, LANES), BF16),
            pltpu.VMEM((CORES, LINE, TC, KK, 2, HALF, LANES), BF16),
            pltpu.VMEM((CORES, LINE, KK, TC, 2, HALF, LANES), BF16),
            dma, dma, dma, dma, dma, dma,
            dma, dma((TC,)), dma, dma((KK,)), dma, dma,
            dma((2, LINE)), dma((LINE, TC)), dma((2, LINE)), dma((LINE, KK)),
            dma((LINE,)), dma, dma((LINE,)), dma((KK,)),
            pltpu.SemaphoreType.REGULAR, pltpu.SemaphoreType.REGULAR, pltpu.SemaphoreType.REGULAR,
        ],
        compiler_params=pltpu.CompilerParams(
            collective_id=0, has_side_effects=True, vmem_limit_bytes=51 * 1024 * 1024),
    )(x, table)


def solution(mesh):
    return jax.shard_map(
        per_device,
        mesh=mesh,
        in_specs=(P(("band", "tr", "tc"), None, None),),
        out_specs=P(("band", "tc"), None, "tr", None),
        check_vma=False,
    )
```

```python
import math

import jax
import jax.numpy as jnp
import ml_dtypes
import numpy as np
from jax import lax
from jax.experimental import pallas as pl
from jax.experimental.pallas import tpu as pltpu
from jax.sharding import PartitionSpec as P

MESH = pl.DeviceIdType.MESH
BF16 = jnp.bfloat16
F32 = jnp.float32

FINE = 32
TAPS = 16
LANES = 128
TC = 8
LINE = 4
CORES = 2
KK = FINE // TC
HOPS = 4
ROWS = HOPS * FINE * 2
OLD = 4
WINDOW = 6
HALF = 16
PART = 4
OFF = (0, 1, 7, 2, 6, 3, 5, 4)
UNITS = TC + KK
ORDER = ((7, 2, (3, 6, 9)), (7, 2, (3, 6, 9)))


def filter_constant():
    length = TAPS * FINE
    offset = (np.arange(length) - (length - 1) / 2.0) / FINE
    prototype = np.sin(math.pi * offset) / (math.pi * offset)
    taps = (prototype / np.sqrt(np.sum(prototype * prototype))).reshape(TAPS, FINE)
    index = np.arange(FINE)
    angle = 2.0 * math.pi * np.mod(index[:, None] * index[None, :], FINE) / FINE
    cosine, sine = np.cos(angle), np.sin(angle)
    fourier = np.zeros((FINE, 2, FINE, 2))
    fourier[:, 0, :, 0] = cosine
    fourier[:, 1, :, 0] = sine
    fourier[:, 0, :, 1] = -sine
    fourier[:, 1, :, 1] = cosine
    table = np.zeros((FINE, 2, 8, WINDOW * HOPS, FINE, 2))
    for s in range(8):
        for t in range(TAPS):
            table[:, :, s, s + 1 + t] = np.transpose(taps[t][:, None, None, None] * fourier, (2, 3, 0, 1))
    table = table.reshape(FINE * 2 * 8, WINDOW * ROWS).astype(np.float32)
    high = table.astype(ml_dtypes.bfloat16)
    low = (table - high.astype(np.float32)).astype(ml_dtypes.bfloat16)
    return np.concatenate([high.reshape(TC, -1, WINDOW * ROWS), low.reshape(TC, -1, WINDOW * ROWS)], axis=1)


def kernel(x_ref, g_hbm, out_ref, g_ref, raw, s_ref, r1, r0, acc,
           g_sem, own_sem, ring_send, ring_recv, halo_send, halo_recv,
           turn1_send, turn1_recv, turn0_send, turn0_recv, own1_sem, own0_sem,
           line1_send, line1_recv, line0_send, line0_recv,
           pair1_send, pair1_recv, pair0_send, pair0_recv,
           line_ok, pair_ok, halo_ok):
    tr = lax.axis_index("tr")
    y = lax.axis_index("tc")
    core = lax.rem(tr, 2)
    zl = tr // 2
    other = 1 - core
    sibling = zl * 2 + other

    table = pltpu.make_async_copy(g_hbm, g_ref, g_sem)
    table.start()

    def at(q, sign):
        return lax.rem(y + sign * OFF[q] + TC, TC)

    barrier = pltpu.get_barrier_semaphore()

    def greet(t, c):
        pl.semaphore_signal(barrier, inc=1, device_id={"tr": t, "tc": c}, device_id_type=MESH)

    for q in range(1, TC):
        greet(tr, at(q, -1))
    last = 2 * LINE - 1
    below = (zl > 0).astype(jnp.int32)
    above = (zl < LINE - 1).astype(jnp.int32)

    @pl.when(core == 1)
    def _():
        @pl.when(zl < LINE - 1)
        def _():
            greet(jnp.minimum(tr + 2, last), y)
            greet(jnp.minimum(tr + 1, last), y)

    @pl.when(core == 0)
    def _():
        @pl.when(zl > 0)
        def _():
            greet(jnp.maximum(tr - 2, 0), y)

    pl.semaphore_wait(barrier, TC - 1 + jnp.where(core == 1, below, 1 + above + below))

    def tell(sem, t):
        pl.semaphore_signal(sem, inc=1, device_id={"tr": t, "tc": y}, device_id_type=MESH)

    @pl.when(core == 1)
    def _():
        @pl.when(zl > 0)
        def _():
            tell(line_ok, jnp.maximum(tr - 2, 0))

    @pl.when(core == 0)
    def _():
        tell(pair_ok, sibling)

        @pl.when(zl > 0)
        def _():
            tell(halo_ok, jnp.maximum(tr - 1, 0))

        @pl.when(zl < LINE - 1)
        def _():
            tell(line_ok, jnp.minimum(tr + 2, last))

    def remote(src, dst, send, recv, t, c):
        return pltpu.make_async_remote_copy(
            src_ref=src, dst_ref=dst, send_sem=send, recv_sem=recv,
            device_id={"tr": t, "tc": c}, device_id_type=MESH)

    for q in range(TC - 1, 0, -1):
        c = at(q, -1)
        remote(x_ref.at[c], raw.at[OLD + y], ring_send, ring_recv, tr, c).start()
    own = pltpu.make_async_copy(x_ref.at[y], raw.at[OLD + y], own_sem)
    own.start()

    @pl.when(tr == 0)
    def _():
        raw[0:OLD] = jnp.zeros((OLD, ROWS, LANES), BF16)

    own.wait()
    arrivals = remote(x_ref.at[pl.ds(0, TC - 1)], raw.at[pl.ds(OLD, TC - 1)], ring_send, ring_recv, tr, y)
    arrivals.wait_send()

    @pl.when(core == 1)
    def _():
        greet(sibling, y)

    arrivals.wait_recv()

    halo = remote(raw.at[pl.ds(TC, OLD)], raw.at[pl.ds(0, OLD)], halo_send, halo_recv, jnp.minimum(tr + 1, last), y)

    @pl.when((core == 1) & (tr < last))
    def _():
        pl.semaphore_wait(halo_ok, 1)

    @pl.when(tr < last)
    def _():
        halo.start()

    table.wait()

    def filterbank(half, after):
        first = HOPS * half
        window = jnp.concatenate(
            [raw[first:first + WINDOW].reshape(WINDOW * ROWS, LANES),
             raw[first + 2:first + 2 + WINDOW].reshape(WINDOW * ROWS, LANES)], axis=1)
        for part in range(2):
            groups = [at(q, -1) for q in range(part * PART, (part + 1) * PART)]
            both = jnp.dot(jnp.concatenate([g_ref[c] for c in groups], axis=0), window, preferred_element_type=F32)
            both = both.reshape(PART, 2, KK * 2, 8, 2 * LANES)
            total = both[:, 0] + both[:, 1]
            pair = jnp.concatenate([total[..., :LANES], total[..., LANES:]], axis=2).astype(BF16)
            for j, c in enumerate(groups):
                s_ref[half, c] = pair[j].reshape(KK, 2, HALF, LANES)
            after(part)

    own1 = pltpu.make_async_copy(s_ref.at[1, y], r1.at[core, zl, y], own1_sem)

    def turn_second(part):
        for q in range(part * PART, (part + 1) * PART):
            if q == 0:
                own1.start()
            else:
                c = at(q, -1)
                remote(s_ref.at[1, c], r1.at[core, zl, y], turn1_send, turn1_recv.at[q], tr, c).start()

    filterbank(1, turn_second)

    def spread(r, s, piece, line_send, line_recv, pair_send, pair_recv, rightward, leftward):
        src = piece(r, s)
        if rightward:
            @pl.when(zl < LINE - 1)
            def _():
                remote(src, src, line_send.at[0, s], line_recv, jnp.minimum(tr + 2, last), y).start()
        if leftward:
            @pl.when(zl > 0)
            def _():
                remote(src, src, line_send.at[1, s], line_recv, jnp.maximum(tr - 2, 0), y).start()
        remote(src, src, pair_send.at[s], pair_recv, sibling, y).start()

    def piece1(q):
        return lambda r, s: r.at[core, s, at(q, 1)]

    def piece0(k):
        return lambda r, s: r.at[core, s, k]

    def from_line(dist, p, r, piece_of, line_send, line_recv, pair_send, pair_recv_of):
        @pl.when(zl >= dist)
        def _():
            s = jnp.maximum(zl - dist, 0)
            piece = piece_of(p)
            remote(piece(r, s), piece(r, s), line_send.at[0, s], line_recv.at[s, p], sibling, y).wait_recv()
            spread(r, s, piece, line_send, line_recv.at[s, p], pair_send, pair_recv_of(s, p), True, False)

        @pl.when(zl < LINE - dist)
        def _():
            s = jnp.minimum(zl + dist, LINE - 1)
            piece = piece_of(p)
            remote(piece(r, s), piece(r, s), line_send.at[1, s], line_recv.at[s, p], sibling, y).wait_recv()
            spread(r, s, piece, line_send, line_recv.at[s, p], pair_send, pair_recv_of(s, p), False, True)

    def pair1_of(s, p):
        return pair1_recv

    def pair0_of(s, p):
        return pair0_recv.at[p]

    def first_half():
        @pl.when(tr > 0)
        def _():
            halo.wait_recv()

        filterbank(0, lambda part: None)
        own0.start()
        for k in range(KK):
            for q in range(1, TC):
                c = at(q, -1)
                remote(s_ref.at[0, c, k], r0.at[core, zl, k, y], turn0_send, turn0_recv.at[k], tr, c).start()

    own0 = pltpu.make_async_copy(s_ref.at[0, y], r0.at[core, zl, :, y], own0_sem)

    def correlation(mine, block):
        swapped = jnp.concatenate([mine[:, :, 1:2], -mine[:, :, 0:1]], axis=2)
        depth = TC * 2 * HALF
        left = jnp.concatenate([mine.reshape(depth, LANES), swapped.reshape(depth, LANES)], axis=1)
        right = jnp.concatenate([block(b).reshape(depth, LANES) for b in range(TC)], axis=1)
        return lax.dot_general(left, right, (((0,), (0,)), ((), ())), preferred_element_type=F32)

    def second(k):
        return correlation(r1[:, :, tr, k], lambda b: r1[:, :, b, k])

    def correlate(k):
        product = acc[...] if k == KK - 1 else second(k)
        product = product + correlation(r0[:, :, k, tr], lambda b: r0[:, :, k, b])
        product = product * (1.0 / (LINE * CORES * 2 * HALF))
        out_ref[k] = product.astype(BF16).reshape(2, LANES, TC * LANES)
        if k == KK - 2:
            acc[...] = second(KK - 1)

    def tail_waits():
        table_half = s_ref.at[1, pl.ds(0, TC - 1)]
        @pl.when(tr < last)
        def _():
            halo.wait_send()

        remote(table_half, table_half, turn1_send, turn1_recv.at[0], sibling, y).wait_send()
        remote(table_half, table_half, turn0_send, turn0_recv.at[0], sibling, y).wait_send()
        sent_waits(r1, line1_send, pair1_send)
        remote(r1.at[other], r1.at[other], pair1_send.at[0], pair1_recv, sibling, y).wait_recv()

    def sent_waits(r, line_send, pair_send):
        for s in range(LINE):
            whole = r.at[core, s]

            @pl.when((zl < LINE - 1) & (s <= zl))
            def _():
                remote(whole, whole, line_send.at[0, s], pair0_recv.at[0], sibling, y).wait_send()

            @pl.when((zl > 0) & (s >= zl))
            def _():
                remote(whole, whole, line_send.at[1, s], pair0_recv.at[0], sibling, y).wait_send()

            remote(whole, whole, pair_send.at[s], pair0_recv.at[0], sibling, y).wait_send()

    def take_own(u):
        if u < TC:
            if u == 0:
                own1.wait()
            else:
                c = at(u, 1)
                remote(s_ref.at[1, 0], r1.at[core, zl, c], turn1_send, turn1_recv.at[u], sibling, y).wait_recv()
            spread(r1, zl, piece1(u), line1_send, line1_recv.at[zl, u], pair1_send, pair1_recv, True, True)
            return
        k = u - TC
        if k == 0:
            own0.wait()
        seven = r0.at[core, zl, k, pl.ds(0, TC - 1)]
        remote(seven, seven, turn0_send, turn0_recv.at[k], sibling, y).wait_recv()
        spread(r0, zl, piece0(k), line0_send, line0_recv.at[zl, k], pair0_send, pair0_recv.at[k], True, True)

    def take_line(dist, u):
        if u < TC:
            from_line(dist, u, r1, piece1, line1_send, line1_recv, pair1_send, pair1_of)
        else:
            from_line(dist, u - TC, r0, piece0, line0_send, line0_recv, pair0_send, pair0_of)

    @pl.when(((core == 1) & (zl < LINE - 1)) | ((core == 0) & (zl > 0)))
    def _():
        pl.semaphore_wait(line_ok, 1)

    @pl.when(core == 1)
    def _():
        pl.semaphore_wait(pair_ok, 1)

    def run(first_at, gap, lag):
        place = [u if u < TC else u + gap for u in range(UNITS)]
        for i in range(place[-1] + lag[2] + 1):
            for u in range(UNITS):
                if place[u] == i:
                    take_own(u)
            if i == first_at:
                first_half()
            for dist in range(1, LINE):
                for u in range(UNITS):
                    if place[u] + lag[dist - 1] == i:
                        take_line(dist, u)
            for k in range(KK):
                if place[TC + k] + lag[2] == i:
                    if k == 0:
                        tail_waits()
                    theirs = r0.at[other, :, k]
                    remote(theirs, theirs, pair0_send.at[0], pair0_recv.at[k], sibling, y).wait_recv()
                    correlate(k)

    @pl.when(core == 1)
    def _():
        run(*ORDER[1])

    @pl.when(core == 0)
    def _():
        run(*ORDER[0])

    sent_waits(r0, line0_send, pair0_send)


def per_device(voltages):
    samples, _, inputs = voltages.shape
    blocks = inputs // LANES
    x = voltages.reshape(samples, 2, blocks, LANES).transpose(2, 0, 1, 3).reshape(blocks, samples * 2, LANES)
    table = jnp.asarray(filter_constant())
    any_spec = pl.BlockSpec(memory_space=pl.ANY)
    dma = pltpu.SemaphoreType.DMA
    return pl.pallas_call(
        kernel,
        out_shape=jax.ShapeDtypeStruct((KK, 2, LANES, inputs), BF16),
        in_specs=[any_spec, pl.BlockSpec(memory_space=pltpu.HBM)],
        out_specs=pl.BlockSpec(memory_space=pltpu.VMEM),
        scratch_shapes=[
            pltpu.VMEM(table.shape, BF16),
            pltpu.VMEM((OLD + TC, ROWS, LANES), BF16),
            pltpu.VMEM((2, TC, KK, 2, HALF, LANES), BF16),
            pltpu.VMEM((CORES, LINE, TC, KK, 2, HALF, LANES), BF16),
            pltpu.VMEM((CORES, LINE, KK, TC, 2, HALF, LANES), BF16),
            pltpu.VMEM((2 * LANES, inputs), F32),
            dma, dma, dma, dma, dma, dma,
            dma, dma((TC,)), dma, dma((KK,)), dma, dma,
            dma((2, LINE)), dma((LINE, TC)), dma((2, LINE)), dma((LINE, KK)),
            dma((LINE,)), dma, dma((LINE,)), dma((KK,)),
            pltpu.SemaphoreType.REGULAR, pltpu.SemaphoreType.REGULAR, pltpu.SemaphoreType.REGULAR,
        ],
        compiler_params=pltpu.CompilerParams(
            collective_id=0, has_side_effects=True, vmem_limit_bytes=51 * 1024 * 1024),
    )(x, table)


def solution(mesh):
    return jax.shard_map(
        per_device,
        mesh=mesh,
        in_specs=(P(("band", "tr", "tc"), None, None),),
        out_specs=P(("band", "tc"), None, "tr", None),
        check_vma=False,
    )
```

```python
import math

import jax
import jax.numpy as jnp
import ml_dtypes
import numpy as np
from jax import lax
from jax.experimental import pallas as pl
from jax.experimental.pallas import tpu as pltpu
from jax.sharding import PartitionSpec as P

MESH = pl.DeviceIdType.MESH
BF16 = jnp.bfloat16
F32 = jnp.float32

FINE = 32
TAPS = 16
LANES = 128
TC = 8
LINE = 4
CORES = 2
KK = FINE // TC
HOPS = 4
ROWS = HOPS * FINE * 2
OLD = 4
WINDOW = 6
HALF = 16
PART = 4
OFF = (0, 1, 7, 2, 6, 3, 5, 4)
UNITS = TC + KK
ORDER = ((4, 2, (3, 6, 9)), (7, 4, (2, 4, 6)))


def filter_constant():
    length = TAPS * FINE
    offset = (np.arange(length) - (length - 1) / 2.0) / FINE
    prototype = np.sin(math.pi * offset) / (math.pi * offset)
    taps = (prototype / np.sqrt(np.sum(prototype * prototype))).reshape(TAPS, FINE)
    index = np.arange(FINE)
    angle = 2.0 * math.pi * np.mod(index[:, None] * index[None, :], FINE) / FINE
    cosine, sine = np.cos(angle), np.sin(angle)
    fourier = np.zeros((FINE, 2, FINE, 2))
    fourier[:, 0, :, 0] = cosine
    fourier[:, 1, :, 0] = sine
    fourier[:, 0, :, 1] = -sine
    fourier[:, 1, :, 1] = cosine
    table = np.zeros((FINE, 2, 8, WINDOW * HOPS, FINE, 2))
    for s in range(8):
        for t in range(TAPS):
            table[:, :, s, s + 1 + t] = np.transpose(taps[t][:, None, None, None] * fourier, (2, 3, 0, 1))
    table = table.reshape(FINE * 2 * 8, WINDOW * ROWS).astype(np.float32)
    high = table.astype(ml_dtypes.bfloat16)
    low = (table - high.astype(np.float32)).astype(ml_dtypes.bfloat16)
    return np.concatenate([high.reshape(TC, -1, WINDOW * ROWS), low.reshape(TC, -1, WINDOW * ROWS)], axis=1)


def kernel(x_ref, g_hbm, out_ref, g_ref, raw, s_ref, r1, r0, acc,
           g_sem, own_sem, ring_send, ring_recv, halo_send, halo_recv,
           turn1_send, turn1_recv, turn0_send, turn0_recv, own1_sem, own0_sem,
           line1_send, line1_recv, line0_send, line0_recv,
           pair1_send, pair1_recv, pair0_send, pair0_recv,
           line_ok, pair_ok, halo_ok):
    tr = lax.axis_index("tr")
    y = lax.axis_index("tc")
    core = lax.rem(tr, 2)
    zl = tr // 2
    other = 1 - core
    sibling = zl * 2 + other

    table = pltpu.make_async_copy(g_hbm, g_ref, g_sem)
    table.start()

    def at(q, sign):
        return lax.rem(y + sign * OFF[q] + TC, TC)

    barrier = pltpu.get_barrier_semaphore()

    def greet(t, c):
        pl.semaphore_signal(barrier, inc=1, device_id={"tr": t, "tc": c}, device_id_type=MESH)

    for q in range(1, TC):
        greet(tr, at(q, -1))
    last = 2 * LINE - 1
    below = (zl > 0).astype(jnp.int32)
    above = (zl < LINE - 1).astype(jnp.int32)

    @pl.when(core == 1)
    def _():
        @pl.when(zl < LINE - 1)
        def _():
            greet(jnp.minimum(tr + 2, last), y)
            greet(jnp.minimum(tr + 1, last), y)

    @pl.when(core == 0)
    def _():
        @pl.when(zl > 0)
        def _():
            greet(jnp.maximum(tr - 2, 0), y)

    pl.semaphore_wait(barrier, TC - 1 + jnp.where(core == 1, below, 1 + above + below))

    def tell(sem, t):
        pl.semaphore_signal(sem, inc=1, device_id={"tr": t, "tc": y}, device_id_type=MESH)

    @pl.when(core == 1)
    def _():
        @pl.when(zl > 0)
        def _():
            tell(line_ok, jnp.maximum(tr - 2, 0))

    @pl.when(core == 0)
    def _():
        tell(pair_ok, sibling)

        @pl.when(zl > 0)
        def _():
            tell(halo_ok, jnp.maximum(tr - 1, 0))

        @pl.when(zl < LINE - 1)
        def _():
            tell(line_ok, jnp.minimum(tr + 2, last))

    def remote(src, dst, send, recv, t, c):
        return pltpu.make_async_remote_copy(
            src_ref=src, dst_ref=dst, send_sem=send, recv_sem=recv,
            device_id={"tr": t, "tc": c}, device_id_type=MESH)

    for q in range(TC - 1, 0, -1):
        c = at(q, -1)
        remote(x_ref.at[c], raw.at[OLD + y], ring_send, ring_recv, tr, c).start()
    own = pltpu.make_async_copy(x_ref.at[y], raw.at[OLD + y], own_sem)
    own.start()

    @pl.when(tr == 0)
    def _():
        raw[0:OLD] = jnp.zeros((OLD, ROWS, LANES), BF16)

    own.wait()
    arrivals = remote(x_ref.at[pl.ds(0, TC - 1)], raw.at[pl.ds(OLD, TC - 1)], ring_send, ring_recv, tr, y)
    arrivals.wait_send()

    @pl.when(core == 1)
    def _():
        greet(sibling, y)

    arrivals.wait_recv()

    halo = remote(raw.at[pl.ds(TC, OLD)], raw.at[pl.ds(0, OLD)], halo_send, halo_recv, jnp.minimum(tr + 1, last), y)

    @pl.when((core == 1) & (tr < last))
    def _():
        pl.semaphore_wait(halo_ok, 1)

    @pl.when(tr < last)
    def _():
        halo.start()

    table.wait()

    def filterbank(half, after):
        first = HOPS * half
        window = jnp.concatenate(
            [raw[first:first + WINDOW].reshape(WINDOW * ROWS, LANES),
             raw[first + 2:first + 2 + WINDOW].reshape(WINDOW * ROWS, LANES)], axis=1)
        for part in range(2):
            groups = [at(q, -1) for q in range(part * PART, (part + 1) * PART)]
            both = jnp.dot(jnp.concatenate([g_ref[c] for c in groups], axis=0), window, preferred_element_type=F32)
            both = both.reshape(PART, 2, KK * 2, 8, 2 * LANES)
            total = both[:, 0] + both[:, 1]
            pair = jnp.concatenate([total[..., :LANES], total[..., LANES:]], axis=2).astype(BF16)
            for j, c in enumerate(groups):
                s_ref[half, c] = pair[j].reshape(KK, 2, HALF, LANES)
            after(part)

    own1 = pltpu.make_async_copy(s_ref.at[1, y], r1.at[core, zl, y], own1_sem)

    def turn_second(part):
        for q in range(part * PART, (part + 1) * PART):
            if q == 0:
                own1.start()
            else:
                c = at(q, -1)
                remote(s_ref.at[1, c], r1.at[core, zl, y], turn1_send, turn1_recv.at[q], tr, c).start()

    filterbank(1, turn_second)

    def spread(r, s, piece, line_send, line_recv, pair_send, pair_recv, rightward, leftward):
        src = piece(r, s)
        if rightward:
            @pl.when(zl < LINE - 1)
            def _():
                remote(src, src, line_send.at[0, s], line_recv, jnp.minimum(tr + 2, last), y).start()
        if leftward:
            @pl.when(zl > 0)
            def _():
                remote(src, src, line_send.at[1, s], line_recv, jnp.maximum(tr - 2, 0), y).start()
        remote(src, src, pair_send.at[s], pair_recv, sibling, y).start()

    def piece1(q):
        return lambda r, s: r.at[core, s, at(q, 1)]

    def piece0(k):
        return lambda r, s: r.at[core, s, k]

    def from_line(dist, p, r, piece_of, line_send, line_recv, pair_send, pair_recv_of):
        @pl.when(zl >= dist)
        def _():
            s = jnp.maximum(zl - dist, 0)
            piece = piece_of(p)
            remote(piece(r, s), piece(r, s), line_send.at[0, s], line_recv.at[s, p], sibling, y).wait_recv()
            spread(r, s, piece, line_send, line_recv.at[s, p], pair_send, pair_recv_of(s, p), True, False)

        @pl.when(zl < LINE - dist)
        def _():
            s = jnp.minimum(zl + dist, LINE - 1)
            piece = piece_of(p)
            remote(piece(r, s), piece(r, s), line_send.at[1, s], line_recv.at[s, p], sibling, y).wait_recv()
            spread(r, s, piece, line_send, line_recv.at[s, p], pair_send, pair_recv_of(s, p), False, True)

    def pair1_of(s, p):
        return pair1_recv

    def pair0_of(s, p):
        return pair0_recv.at[p]

    def first_half():
        @pl.when(tr > 0)
        def _():
            halo.wait_recv()

        filterbank(0, lambda part: None)
        own0.start()
        for k in range(KK):
            for q in range(1, TC):
                c = at(q, -1)
                remote(s_ref.at[0, c, k], r0.at[core, zl, k, y], turn0_send, turn0_recv.at[k], tr, c).start()

    own0 = pltpu.make_async_copy(s_ref.at[0, y], r0.at[core, zl, :, y], own0_sem)

    def correlation(mine, block):
        swapped = jnp.concatenate([mine[:, :, 1:2], -mine[:, :, 0:1]], axis=2)
        depth = TC * 2 * HALF
        left = jnp.concatenate([mine.reshape(depth, LANES), swapped.reshape(depth, LANES)], axis=1)
        right = jnp.concatenate([block(b).reshape(depth, LANES) for b in range(TC)], axis=1)
        return lax.dot_general(left, right, (((0,), (0,)), ((), ())), preferred_element_type=F32)

    def second(k):
        return correlation(r1[:, :, tr, k], lambda b: r1[:, :, b, k])

    def correlate(k):
        product = acc[...] if k == KK - 1 else second(k)
        product = product + correlation(r0[:, :, k, tr], lambda b: r0[:, :, k, b])
        product = product * (1.0 / (LINE * CORES * 2 * HALF))
        out_ref[k] = product.astype(BF16).reshape(2, LANES, TC * LANES)
        if k == KK - 2:
            acc[...] = second(KK - 1)

    def tail_waits():
        table_half = s_ref.at[1, pl.ds(0, TC - 1)]
        @pl.when(tr < last)
        def _():
            halo.wait_send()

        remote(table_half, table_half, turn1_send, turn1_recv.at[0], sibling, y).wait_send()
        remote(table_half, table_half, turn0_send, turn0_recv.at[0], sibling, y).wait_send()
        sent_waits(r1, line1_send, pair1_send)
        remote(r1.at[other], r1.at[other], pair1_send.at[0], pair1_recv, sibling, y).wait_recv()

    def sent_waits(r, line_send, pair_send):
        for s in range(LINE):
            whole = r.at[core, s]

            @pl.when((zl < LINE - 1) & (s <= zl))
            def _():
                remote(whole, whole, line_send.at[0, s], pair0_recv.at[0], sibling, y).wait_send()

            @pl.when((zl > 0) & (s >= zl))
            def _():
                remote(whole, whole, line_send.at[1, s], pair0_recv.at[0], sibling, y).wait_send()

            remote(whole, whole, pair_send.at[s], pair0_recv.at[0], sibling, y).wait_send()

    def take_own(u):
        if u < TC:
            if u == 0:
                own1.wait()
            else:
                c = at(u, 1)
                remote(s_ref.at[1, 0], r1.at[core, zl, c], turn1_send, turn1_recv.at[u], sibling, y).wait_recv()
            spread(r1, zl, piece1(u), line1_send, line1_recv.at[zl, u], pair1_send, pair1_recv, True, True)
            return
        k = u - TC
        if k == 0:
            own0.wait()
        seven = r0.at[core, zl, k, pl.ds(0, TC - 1)]
        remote(seven, seven, turn0_send, turn0_recv.at[k], sibling, y).wait_recv()
        spread(r0, zl, piece0(k), line0_send, line0_recv.at[zl, k], pair0_send, pair0_recv.at[k], True, True)

    def take_line(dist, u):
        if u < TC:
            from_line(dist, u, r1, piece1, line1_send, line1_recv, pair1_send, pair1_of)
        else:
            from_line(dist, u - TC, r0, piece0, line0_send, line0_recv, pair0_send, pair0_of)

    @pl.when(((core == 1) & (zl < LINE - 1)) | ((core == 0) & (zl > 0)))
    def _():
        pl.semaphore_wait(line_ok, 1)

    @pl.when(core == 1)
    def _():
        pl.semaphore_wait(pair_ok, 1)

    def run(first_at, gap, lag):
        place = [u if u < TC else u + gap for u in range(UNITS)]
        for i in range(place[-1] + lag[2] + 1):
            for u in range(UNITS):
                if place[u] == i:
                    take_own(u)
            if i == first_at:
                first_half()
            for dist in range(1, LINE):
                for u in range(UNITS):
                    if place[u] + lag[dist - 1] == i:
                        take_line(dist, u)
            for k in range(KK):
                if place[TC + k] + lag[2] == i:
                    if k == 0:
                        tail_waits()
                    theirs = r0.at[other, :, k]
                    remote(theirs, theirs, pair0_send.at[0], pair0_recv.at[k], sibling, y).wait_recv()
                    correlate(k)

    @pl.when(core == 1)
    def _():
        run(*ORDER[1])

    @pl.when(core == 0)
    def _():
        run(*ORDER[0])

    sent_waits(r0, line0_send, pair0_send)


def per_device(voltages):
    samples, _, inputs = voltages.shape
    blocks = inputs // LANES
    x = voltages.reshape(samples, 2, blocks, LANES).transpose(2, 0, 1, 3).reshape(blocks, samples * 2, LANES)
    table = jnp.asarray(filter_constant())
    any_spec = pl.BlockSpec(memory_space=pl.ANY)
    dma = pltpu.SemaphoreType.DMA
    return pl.pallas_call(
        kernel,
        out_shape=jax.ShapeDtypeStruct((KK, 2, LANES, inputs), BF16),
        in_specs=[any_spec, pl.BlockSpec(memory_space=pltpu.HBM)],
        out_specs=pl.BlockSpec(memory_space=pltpu.VMEM),
        scratch_shapes=[
            pltpu.VMEM(table.shape, BF16),
            pltpu.VMEM((OLD + TC, ROWS, LANES), BF16),
            pltpu.VMEM((2, TC, KK, 2, HALF, LANES), BF16),
            pltpu.VMEM((CORES, LINE, TC, KK, 2, HALF, LANES), BF16),
            pltpu.VMEM((CORES, LINE, KK, TC, 2, HALF, LANES), BF16),
            pltpu.VMEM((2 * LANES, inputs), F32),
            dma, dma, dma, dma, dma, dma,
            dma, dma((TC,)), dma, dma((KK,)), dma, dma,
            dma((2, LINE)), dma((LINE, TC)), dma((2, LINE)), dma((LINE, KK)),
            dma((LINE,)), dma, dma((LINE,)), dma((KK,)),
            pltpu.SemaphoreType.REGULAR, pltpu.SemaphoreType.REGULAR, pltpu.SemaphoreType.REGULAR,
        ],
        compiler_params=pltpu.CompilerParams(
            collective_id=0, has_side_effects=True, vmem_limit_bytes=51 * 1024 * 1024),
    )(x, table)


def solution(mesh):
    return jax.shard_map(
        per_device,
        mesh=mesh,
        in_specs=(P(("band", "tr", "tc"), None, None),),
        out_specs=P(("band", "tc"), None, "tr", None),
        check_vma=False,
    )
```

```python
import math

import jax
import jax.numpy as jnp
import ml_dtypes
import numpy as np
from jax import lax
from jax.experimental import pallas as pl
from jax.experimental.pallas import tpu as pltpu
from jax.sharding import PartitionSpec as P

MESH = pl.DeviceIdType.MESH
BF16 = jnp.bfloat16
F32 = jnp.float32

FINE = 32
TAPS = 16
LANES = 128
TC = 8
LINE = 4
CORES = 2
KK = FINE // TC
HOPS = 4
ROWS = HOPS * FINE * 2
OLD = 4
WINDOW = 6
HALF = 16
PART = 4
OFF = (0, 1, 7, 2, 6, 3, 5, 4)
UNITS = TC + KK
ORDER = ((7, 0, (3, 6, 9)), (7, 2, (3, 6, 9)))


def filter_constant():
    length = TAPS * FINE
    offset = (np.arange(length) - (length - 1) / 2.0) / FINE
    prototype = np.sin(math.pi * offset) / (math.pi * offset)
    taps = (prototype / np.sqrt(np.sum(prototype * prototype))).reshape(TAPS, FINE)
    index = np.arange(FINE)
    angle = 2.0 * math.pi * np.mod(index[:, None] * index[None, :], FINE) / FINE
    cosine, sine = np.cos(angle), np.sin(angle)
    fourier = np.zeros((FINE, 2, FINE, 2))
    fourier[:, 0, :, 0] = cosine
    fourier[:, 1, :, 0] = sine
    fourier[:, 0, :, 1] = -sine
    fourier[:, 1, :, 1] = cosine
    table = np.zeros((FINE, 2, 8, WINDOW * HOPS, FINE, 2))
    for s in range(8):
        for t in range(TAPS):
            table[:, :, s, s + 1 + t] = np.transpose(taps[t][:, None, None, None] * fourier, (2, 3, 0, 1))
    table = table.reshape(FINE * 2 * 8, WINDOW * ROWS).astype(np.float32)
    high = table.astype(ml_dtypes.bfloat16)
    low = (table - high.astype(np.float32)).astype(ml_dtypes.bfloat16)
    return np.concatenate([high.reshape(TC, -1, WINDOW * ROWS), low.reshape(TC, -1, WINDOW * ROWS)], axis=1)


def kernel(x_ref, g_hbm, out_ref, g_ref, raw, s_ref, r1, r0, acc,
           g_sem, own_sem, ring_send, ring_recv, halo_send, halo_recv,
           turn1_send, turn1_recv, turn0_send, turn0_recv, own1_sem, own0_sem,
           line1_send, line1_recv, line0_send, line0_recv,
           pair1_send, pair1_recv, pair0_send, pair0_recv,
           line_ok, pair_ok, halo_ok):
    tr = lax.axis_index("tr")
    y = lax.axis_index("tc")
    core = lax.rem(tr, 2)
    zl = tr // 2
    other = 1 - core
    sibling = zl * 2 + other

    table = pltpu.make_async_copy(g_hbm, g_ref, g_sem)
    table.start()

    def at(q, sign):
        return lax.rem(y + sign * OFF[q] + TC, TC)

    barrier = pltpu.get_barrier_semaphore()

    def greet(t, c):
        pl.semaphore_signal(barrier, inc=1, device_id={"tr": t, "tc": c}, device_id_type=MESH)

    for q in range(1, TC):
        greet(tr, at(q, -1))
    last = 2 * LINE - 1
    below = (zl > 0).astype(jnp.int32)
    above = (zl < LINE - 1).astype(jnp.int32)

    @pl.when(core == 1)
    def _():
        @pl.when(zl < LINE - 1)
        def _():
            greet(jnp.minimum(tr + 2, last), y)
            greet(jnp.minimum(tr + 1, last), y)

    @pl.when(core == 0)
    def _():
        @pl.when(zl > 0)
        def _():
            greet(jnp.maximum(tr - 2, 0), y)

    pl.semaphore_wait(barrier, TC - 1 + jnp.where(core == 1, below, 1 + above + below))

    def tell(sem, t):
        pl.semaphore_signal(sem, inc=1, device_id={"tr": t, "tc": y}, device_id_type=MESH)

    @pl.when(core == 1)
    def _():
        @pl.when(zl > 0)
        def _():
            tell(line_ok, jnp.maximum(tr - 2, 0))

    @pl.when(core == 0)
    def _():
        tell(pair_ok, sibling)

        @pl.when(zl > 0)
        def _():
            tell(halo_ok, jnp.maximum(tr - 1, 0))

        @pl.when(zl < LINE - 1)
        def _():
            tell(line_ok, jnp.minimum(tr + 2, last))

    def remote(src, dst, send, recv, t, c):
        return pltpu.make_async_remote_copy(
            src_ref=src, dst_ref=dst, send_sem=send, recv_sem=recv,
            device_id={"tr": t, "tc": c}, device_id_type=MESH)

    for q in range(TC - 1, 0, -1):
        c = at(q, -1)
        remote(x_ref.at[c], raw.at[OLD + y], ring_send, ring_recv, tr, c).start()
    own = pltpu.make_async_copy(x_ref.at[y], raw.at[OLD + y], own_sem)
    own.start()

    @pl.when(tr == 0)
    def _():
        raw[0:OLD] = jnp.zeros((OLD, ROWS, LANES), BF16)

    own.wait()
    arrivals = remote(x_ref.at[pl.ds(0, TC - 1)], raw.at[pl.ds(OLD, TC - 1)], ring_send, ring_recv, tr, y)
    arrivals.wait_send()

    @pl.when(core == 1)
    def _():
        greet(sibling, y)

    arrivals.wait_recv()

    halo = remote(raw.at[pl.ds(TC, OLD)], raw.at[pl.ds(0, OLD)], halo_send, halo_recv, jnp.minimum(tr + 1, last), y)

    @pl.when((core == 1) & (tr < last))
    def _():
        pl.semaphore_wait(halo_ok, 1)

    @pl.when(tr < last)
    def _():
        halo.start()

    table.wait()

    def filterbank(half, after):
        first = HOPS * half
        window = jnp.concatenate(
            [raw[first:first + WINDOW].reshape(WINDOW * ROWS, LANES),
             raw[first + 2:first + 2 + WINDOW].reshape(WINDOW * ROWS, LANES)], axis=1)
        for part in range(2):
            groups = [at(q, -1) for q in range(part * PART, (part + 1) * PART)]
            both = jnp.dot(jnp.concatenate([g_ref[c] for c in groups], axis=0), window, preferred_element_type=F32)
            both = both.reshape(PART, 2, KK * 2, 8, 2 * LANES)
            total = both[:, 0] + both[:, 1]
            pair = jnp.concatenate([total[..., :LANES], total[..., LANES:]], axis=2).astype(BF16)
            for j, c in enumerate(groups):
                s_ref[half, c] = pair[j].reshape(KK, 2, HALF, LANES)
            after(part)

    own1 = pltpu.make_async_copy(s_ref.at[1, y], r1.at[core, zl, y], own1_sem)

    def turn_second(part):
        for q in range(part * PART, (part + 1) * PART):
            if q == 0:
                own1.start()
            else:
                c = at(q, -1)
                remote(s_ref.at[1, c], r1.at[core, zl, y], turn1_send, turn1_recv.at[q], tr, c).start()

    filterbank(1, turn_second)

    def spread(r, s, piece, line_send, line_recv, pair_send, pair_recv, rightward, leftward):
        src = piece(r, s)
        if rightward:
            @pl.when(zl < LINE - 1)
            def _():
                remote(src, src, line_send.at[0, s], line_recv, jnp.minimum(tr + 2, last), y).start()
        if leftward:
            @pl.when(zl > 0)
            def _():
                remote(src, src, line_send.at[1, s], line_recv, jnp.maximum(tr - 2, 0), y).start()
        remote(src, src, pair_send.at[s], pair_recv, sibling, y).start()

    def piece1(q):
        return lambda r, s: r.at[core, s, at(q, 1)]

    def piece0(k):
        return lambda r, s: r.at[core, s, k]

    def from_line(dist, p, r, piece_of, line_send, line_recv, pair_send, pair_recv_of):
        @pl.when(zl >= dist)
        def _():
            s = jnp.maximum(zl - dist, 0)
            piece = piece_of(p)
            remote(piece(r, s), piece(r, s), line_send.at[0, s], line_recv.at[s, p], sibling, y).wait_recv()
            spread(r, s, piece, line_send, line_recv.at[s, p], pair_send, pair_recv_of(s, p), True, False)

        @pl.when(zl < LINE - dist)
        def _():
            s = jnp.minimum(zl + dist, LINE - 1)
            piece = piece_of(p)
            remote(piece(r, s), piece(r, s), line_send.at[1, s], line_recv.at[s, p], sibling, y).wait_recv()
            spread(r, s, piece, line_send, line_recv.at[s, p], pair_send, pair_recv_of(s, p), False, True)

    def pair1_of(s, p):
        return pair1_recv

    def pair0_of(s, p):
        return pair0_recv.at[p]

    def first_half():
        @pl.when(tr > 0)
        def _():
            halo.wait_recv()

        filterbank(0, lambda part: None)
        own0.start()
        for k in range(KK):
            for q in range(1, TC):
                c = at(q, -1)
                remote(s_ref.at[0, c, k], r0.at[core, zl, k, y], turn0_send, turn0_recv.at[k], tr, c).start()

    own0 = pltpu.make_async_copy(s_ref.at[0, y], r0.at[core, zl, :, y], own0_sem)

    def correlation(mine, block):
        swapped = jnp.concatenate([mine[:, :, 1:2], -mine[:, :, 0:1]], axis=2)
        depth = TC * 2 * HALF
        left = jnp.concatenate([mine.reshape(depth, LANES), swapped.reshape(depth, LANES)], axis=1)
        right = jnp.concatenate([block(b).reshape(depth, LANES) for b in range(TC)], axis=1)
        return lax.dot_general(left, right, (((0,), (0,)), ((), ())), preferred_element_type=F32)

    def second(k):
        return correlation(r1[:, :, tr, k], lambda b: r1[:, :, b, k])

    def correlate(k):
        product = acc[...] if k == KK - 1 else second(k)
        product = product + correlation(r0[:, :, k, tr], lambda b: r0[:, :, k, b])
        product = product * (1.0 / (LINE * CORES * 2 * HALF))
        out_ref[k] = product.astype(BF16).reshape(2, LANES, TC * LANES)
        if k == KK - 2:
            acc[...] = second(KK - 1)

    def tail_waits():
        table_half = s_ref.at[1, pl.ds(0, TC - 1)]
        @pl.when(tr < last)
        def _():
            halo.wait_send()

        remote(table_half, table_half, turn1_send, turn1_recv.at[0], sibling, y).wait_send()
        remote(table_half, table_half, turn0_send, turn0_recv.at[0], sibling, y).wait_send()
        sent_waits(r1, line1_send, pair1_send)
        remote(r1.at[other], r1.at[other], pair1_send.at[0], pair1_recv, sibling, y).wait_recv()

    def sent_waits(r, line_send, pair_send):
        for s in range(LINE):
            whole = r.at[core, s]

            @pl.when((zl < LINE - 1) & (s <= zl))
            def _():
                remote(whole, whole, line_send.at[0, s], pair0_recv.at[0], sibling, y).wait_send()

            @pl.when((zl > 0) & (s >= zl))
            def _():
                remote(whole, whole, line_send.at[1, s], pair0_recv.at[0], sibling, y).wait_send()

            remote(whole, whole, pair_send.at[s], pair0_recv.at[0], sibling, y).wait_send()

    def take_own(u):
        if u < TC:
            if u == 0:
                own1.wait()
            else:
                c = at(u, 1)
                remote(s_ref.at[1, 0], r1.at[core, zl, c], turn1_send, turn1_recv.at[u], sibling, y).wait_recv()
            spread(r1, zl, piece1(u), line1_send, line1_recv.at[zl, u], pair1_send, pair1_recv, True, True)
            return
        k = u - TC
        if k == 0:
            own0.wait()
        seven = r0.at[core, zl, k, pl.ds(0, TC - 1)]
        remote(seven, seven, turn0_send, turn0_recv.at[k], sibling, y).wait_recv()
        spread(r0, zl, piece0(k), line0_send, line0_recv.at[zl, k], pair0_send, pair0_recv.at[k], True, True)

    def take_line(dist, u):
        if u < TC:
            from_line(dist, u, r1, piece1, line1_send, line1_recv, pair1_send, pair1_of)
        else:
            from_line(dist, u - TC, r0, piece0, line0_send, line0_recv, pair0_send, pair0_of)

    @pl.when(((core == 1) & (zl < LINE - 1)) | ((core == 0) & (zl > 0)))
    def _():
        pl.semaphore_wait(line_ok, 1)

    @pl.when(core == 1)
    def _():
        pl.semaphore_wait(pair_ok, 1)

    def run(first_at, gap, lag):
        place = [u if u < TC else u + gap for u in range(UNITS)]
        for i in range(place[-1] + lag[2] + 1):
            for u in range(UNITS):
                if place[u] == i:
                    take_own(u)
            if i == first_at:
                first_half()
            for dist in range(1, LINE):
                for u in range(UNITS):
                    if place[u] + lag[dist - 1] == i:
                        take_line(dist, u)
            for k in range(KK):
                if place[TC + k] + lag[2] == i:
                    if k == 0:
                        tail_waits()
                    theirs = r0.at[other, :, k]
                    remote(theirs, theirs, pair0_send.at[0], pair0_recv.at[k], sibling, y).wait_recv()
                    correlate(k)

    @pl.when(core == 1)
    def _():
        run(*ORDER[1])

    @pl.when(core == 0)
    def _():
        run(*ORDER[0])

    sent_waits(r0, line0_send, pair0_send)


def per_device(voltages):
    samples, _, inputs = voltages.shape
    blocks = inputs // LANES
    x = voltages.reshape(samples, 2, blocks, LANES).transpose(2, 0, 1, 3).reshape(blocks, samples * 2, LANES)
    table = jnp.asarray(filter_constant())
    any_spec = pl.BlockSpec(memory_space=pl.ANY)
    dma = pltpu.SemaphoreType.DMA
    return pl.pallas_call(
        kernel,
        out_shape=jax.ShapeDtypeStruct((KK, 2, LANES, inputs), BF16),
        in_specs=[any_spec, pl.BlockSpec(memory_space=pltpu.HBM)],
        out_specs=pl.BlockSpec(memory_space=pltpu.VMEM),
        scratch_shapes=[
            pltpu.VMEM(table.shape, BF16),
            pltpu.VMEM((OLD + TC, ROWS, LANES), BF16),
            pltpu.VMEM((2, TC, KK, 2, HALF, LANES), BF16),
            pltpu.VMEM((CORES, LINE, TC, KK, 2, HALF, LANES), BF16),
            pltpu.VMEM((CORES, LINE, KK, TC, 2, HALF, LANES), BF16),
            pltpu.VMEM((2 * LANES, inputs), F32),
            dma, dma, dma, dma, dma, dma,
            dma, dma((TC,)), dma, dma((KK,)), dma, dma,
            dma((2, LINE)), dma((LINE, TC)), dma((2, LINE)), dma((LINE, KK)),
            dma((LINE,)), dma, dma((LINE,)), dma((KK,)),
            pltpu.SemaphoreType.REGULAR, pltpu.SemaphoreType.REGULAR, pltpu.SemaphoreType.REGULAR,
        ],
        compiler_params=pltpu.CompilerParams(
            collective_id=0, has_side_effects=True, vmem_limit_bytes=51 * 1024 * 1024),
    )(x, table)


def solution(mesh):
    return jax.shard_map(
        per_device,
        mesh=mesh,
        in_specs=(P(("band", "tr", "tc"), None, None),),
        out_specs=P(("band", "tc"), None, "tr", None),
        check_vma=False,
    )
```
